256 devices in a mesh: row: 32 (over z, y_hi, core), col: 8 (over x, y_lo).
Axes of the slice: x: 4, y: 4 (y_hi: 2, y_lo: 2; y = y_hi * 2 + y_lo), z: 8, core: 2. Of those that a mesh axis runs over, the one named last changes fastest.
Arguments:
- seq: float32 [1536, 1024], P('row', 'col'), may hold values from -6 to 6
- query: float32 [1536, 1024], P('row', 'col'), may hold values from -24 to 24, as said below
- key: float32 [1536, 1024], P('col', 'row'), may hold values from -24 to 24, as said below
- value: float32 [1536, 1024], P('col', 'row'), may hold values from -6 to 6
- pair: float32 [1536, 1536, 128], P('row', 'col'), may hold values from -6 to 6
- w_bias: float32 [128, 32], replicated, may hold values from -0.5 to 0.5
- w_out: float32 [1024, 1024], P(None, 'col'), may hold values from -0.75 to 0.75
- w_left: float32 [1024, 64], P('col'), may hold values from -0.1875 to 0.1875
- w_right: float32 [1024, 64], P('col'), may hold values from -0.1875 to 0.1875
- w_outer: float32 [128, 128], replicated, may hold values from -0.5 to 0.5
- outer_bias: float32 [128], replicated, may hold values from -3 to 3
- w_up: float32 [128, 512], replicated, may hold values from -0.5 to 0.5
- w_down: float32 [512, 128], replicated, may hold values from -0.25 to 0.25
Outputs:
- seq_new: float32 [1536, 1024], P('row', 'col')
- pair_new: float32 [1536, 1536, 128], P('row', 'col')
The draws below stay inside these ranges and needn't reach their ends.
Inputs may be any that keep to these rules, and one draw needn't show every extreme that they name: `query`: Head-major queries of order one; some residues may be much larger. `key`: Head-major keys of order one; some residues may be much larger.
All inputs are finite; a program needn't handle non-finite values.
Results may differ from the reference program's by a relative error of at most 0.0003.
Values sent between devices are 32-bit elements; how exact they have to be, the bound alone decides.
No kernel may reach another device: no remote copies, remote signals or barrier semaphores. Data moves between devices by JAX's collectives and lax.ppermute only.
A program may use at most 64 MiB of HBM per device.

```python
import jax
import jax.numpy as jnp
from jax import lax

HEADS = 32
CP = 128
PAIR_HIDDEN = 512
OPD = 64
RES = 48
D = 1024
RESIDUES = 1536
N_ROW = 32


def draw_shared(key):
    base = jax.random.fold_in(key, 77)
    first, second = jax.random.split(base, 2)
    queries = jnp.clip(jax.random.normal(first, (RESIDUES, D), jnp.float32), -6.0, 6.0)
    keys_drawn = jnp.clip(jax.random.normal(second, (RESIDUES, D), jnp.float32), -6.0, 6.0)
    return (queries, keys_drawn)


def draw_query(key, part):
    return draw_shared(key)[0]


def draw_key(key, part):
    return draw_shared(key)[1]


def block_levels(key, dims, shards, least, largest):
    def one(position, shards_of):
        steps = jax.random.uniform(jax.random.fold_in(jax.random.fold_in(key, 6), position), (shards_of,), jnp.float32, least / len(shards), largest / len(shards))
        return jnp.repeat(jnp.exp(steps), dims[position] // shards_of).reshape((-1,) + (1,) * (len(dims) - position - 1))

    gain = one(*shards[0])
    for cut in shards[1:]:
        gain = gain * one(*cut)
    return gain


def noise(own_key, extent, deviation, bound, shards=(), dtype=jnp.bfloat16):
    level = block_levels(own_key, extent, shards, -0.22, 0.18) if shards else 1.0
    drawn = jax.random.normal(own_key, extent, jnp.float32) * deviation * level
    return jnp.minimum(jnp.maximum(drawn, -bound), bound).astype(dtype)


def setup_inputs(seed: int = 0) -> dict:
    splits = jax.random.split(jax.random.key(seed), 14)
    seq = noise(splits[0], (RESIDUES, D), 1.0, 6.0, ((0, 32), (1, 8)), jnp.float32)
    query = draw_query(jax.random.fold_in(splits[13], 71), 0)
    key = draw_key(jax.random.fold_in(splits[13], 71), 0)
    value = noise(splits[3], (RESIDUES, D), 1.0, 6.0, ((0, 8), (1, 32)), jnp.float32)
    pair = noise(splits[4], (RESIDUES, RESIDUES, CP), 1.0, 6.0, ((0, 32), (1, 8)), jnp.float32)
    w_bias = noise(splits[5], (CP, HEADS), CP ** -0.5, 0.5, (), jnp.float32)
    w_out = noise(splits[6], (D, D), (D // 16) ** -0.5, 0.75, ((1, 8),), jnp.float32)
    w_left = noise(splits[7], (D, OPD), D ** -0.5, 0.1875, ((0, 8),), jnp.float32)
    w_right = noise(splits[8], (D, OPD), D ** -0.5, 0.1875, ((0, 8),), jnp.float32)
    w_outer = noise(splits[9], (2 * OPD, CP), (2 * OPD) ** -0.5, 0.5, (), jnp.float32)
    outer_bias = noise(splits[10], (CP,), 0.5, 3.0, (), jnp.float32)
    w_up = noise(splits[11], (CP, PAIR_HIDDEN), CP ** -0.5, 0.5, (), jnp.float32)
    w_down = noise(splits[12], (PAIR_HIDDEN, CP), PAIR_HIDDEN ** -0.5, 0.25, (), jnp.float32)
    return {"seq": seq, "query": query, "key": key, "value": value, "pair": pair, "w_bias": w_bias, "w_out": w_out, "w_left": w_left, "w_right": w_right, "w_outer": w_outer, "outer_bias": outer_bias, "w_up": w_up, "w_down": w_down}


HIGH = lax.Precision.HIGHEST

def channel_norm(x):
    centre = x - lax.optimization_barrier(jnp.mean(x, axis=-1, keepdims=True))
    return centre * lax.rsqrt(lax.optimization_barrier(jnp.mean(centre * centre, axis=-1, keepdims=True)) + 1e-05)

def reference(seq, query, key, value, pair, w_bias, w_out, w_left, w_right, w_outer, outer_bias, w_up, w_down):
    residues = seq.shape[0]
    heads = w_bias.shape[1]
    head_dim = seq.shape[1] // heads
    proj_width = w_left.shape[1]
    blocks = pair.reshape(N_ROW, RES, residues, pair.shape[2])

    def make_bias(block):
        return jnp.einsum('ijc,ch->ihj', channel_norm(block), w_bias, precision=HIGH)
    bias = lax.map(make_bias, blocks).reshape(residues, heads, residues)
    q_heads = query.reshape(residues, heads, head_dim)
    k_heads = key.reshape(residues, heads, head_dim)
    v_heads = value.reshape(residues, heads, head_dim)
    scores = jnp.einsum('ihd,jhd->ihj', q_heads, k_heads, precision=HIGH) / jnp.sqrt(jnp.float32(head_dim)) + bias
    weights = jax.nn.softmax(scores, axis=-1)
    attn = jnp.einsum('ihj,jhd->ihd', weights, v_heads, precision=HIGH).reshape(residues, heads * head_dim)
    seq_new = seq + jnp.dot(attn, w_out, precision=HIGH)
    mean_value = lax.optimization_barrier(jnp.mean(seq_new, axis=1, keepdims=True))
    mean_square = lax.optimization_barrier(jnp.mean(seq_new * seq_new, axis=1, keepdims=True))
    seq_norm = (seq_new - mean_value) * lax.rsqrt(mean_square - mean_value * mean_value + 1e-05)
    left = jnp.dot(seq_norm, w_left, precision=HIGH)
    right = jnp.dot(seq_norm, w_right, precision=HIGH)
    w_prod = w_outer[:proj_width]
    w_diff = w_outer[proj_width:]
    table = right[:, :, None] * w_prod[None, :, :]
    right_diff = jnp.dot(right, w_diff, precision=HIGH)
    left_diff = jnp.dot(left, w_diff, precision=HIGH)
    left_blocks = left.reshape(N_ROW, RES, proj_width)
    left_diff_blocks = left_diff.reshape(N_ROW, RES, left_diff.shape[1])

    def update(args):
        block, left_block, diff_block = args
        outer = jnp.einsum('ip,jpc->ijc', left_block, table, precision=HIGH) + diff_block[:, None, :] - right_diff[None, :, :] + outer_bias
        mid = block + outer
        hidden_act = jax.nn.relu(jnp.einsum('ijc,ck->ijk', channel_norm(mid), w_up, precision=HIGH))
        return mid + jnp.einsum('ijk,kc->ijc', hidden_act, w_down, precision=HIGH)
    pair_new = lax.map(update, (blocks, left_blocks, left_diff_blocks)).reshape(pair.shape)
    return (seq_new, pair_new)
```

```python
import functools

import jax
import jax.numpy as jnp
from jax import lax
from jax.experimental import pallas as pl
from jax.experimental.pallas import tpu as pltpu
from jax.sharding import PartitionSpec as P

HIGH = lax.Precision.HIGHEST
EPS = 1e-05
BF = jnp.bfloat16
F32 = jnp.float32
ROWS_PER_STEP = 4


def dot(a, b, dims=((1,), (0,)), precision=HIGH):
    return lax.dot_general(a, b, (dims, ((), ())), precision=precision, preferred_element_type=F32)


def bdot(a, b):
    return lax.dot_general(a, b, (((1,), (0,)), ((), ())), preferred_element_type=F32)


def channel_norm(x):
    centre = x - jnp.mean(x, axis=-1, keepdims=True)
    return centre * lax.rsqrt(jnp.mean(centre * centre, axis=-1, keepdims=True) + EPS)


def split(x):
    high = lax.reduce_precision(x, 8, 7)
    return high.astype(BF), (x - high).astype(BF)


def ksplit(x):
    high = x.astype(BF)
    return high, (x - high.astype(F32)).astype(BF)


def merge_kernel(heads_per, parts_ref, out_ref):
    sources, _, lanes = parts_ref.shape
    rows = out_ref.shape[1]
    tops = [parts_ref[s, rows : rows + 8, :] for s in range(sources)]
    top = functools.reduce(jnp.maximum, [t[:heads_per] for t in tops])
    scales = [jnp.exp(t[:heads_per] - top) for t in tops]
    total = sum(t[heads_per : 2 * heads_per] * s for t, s in zip(tops, scales))
    row = lax.broadcasted_iota(jnp.int32, (heads_per, lanes), 0)
    lane = lax.broadcasted_iota(jnp.int32, (heads_per, lanes), 1)
    spread = (lane // (lanes // heads_per) == row).astype(F32)
    attn = jnp.zeros((rows, lanes), F32)
    for s in range(sources):
        factor = dot(scales[s] / total, spread, ((0,), (0,)))
        attn = attn + parts_ref[s, :rows, :] * factor[:rows]
    for s in range(sources):
        out_ref[s] = attn


def project_kernel(attn_ref, w_out_ref, seq_ref, w_lr_ref, seq_new_ref, out_ref):
    sources, rows, lanes = attn_ref.shape
    total = seq_ref[...]
    for s in range(sources):
        total = total + dot(attn_ref[s], w_out_ref[s * lanes : (s + 1) * lanes, :])
    seq_new_ref[...] = total
    w_lr = w_lr_ref[...]
    part = dot(total, w_lr)
    ones = jnp.ones((8, lanes), F32)
    sums = dot(ones, total, ((1,), (1,)))
    squares = dot(ones, total * total, ((1,), (1,)))
    row = lax.broadcasted_iota(jnp.int32, (8, rows), 0)
    stats = jnp.where(row == 0, sums, squares)
    columns = jnp.sum(w_lr, axis=0, keepdims=True)
    for s in range(out_ref.shape[0]):
        out_ref[s, :rows, :] = part
        out_ref[s, rows : rows + 8, :] = jnp.zeros((8, lanes), F32)
        out_ref[s, rows : rows + 2, :rows] = stats[:2]
        out_ref[s, rows + 2 : rows + 3, :] = columns


def left_right_kernel(width, parts_ref, left_ref, right_ref):
    sources = parts_ref.shape[0]
    rows, lanes = left_ref.shape
    total = parts_ref[0]
    for s in range(1, sources):
        total = total + parts_ref[s]
    stats = jnp.transpose(total[rows : rows + 8, :])
    mean = stats[:rows, 0:1] / width
    square = stats[:rows, 1:2] / width
    both = (total[:rows] - mean * total[rows + 2 : rows + 3]) * lax.rsqrt(square - mean * mean + EPS)
    swapped = pltpu.roll(both, lanes // 2, 1)
    first = lax.broadcasted_iota(jnp.int32, (rows, lanes), 1) < lanes // 2
    left_ref[...] = jnp.where(first, both, swapped)
    right = jnp.where(first, swapped, both)
    packed = jnp.where(first[: rows // 2], right[: rows // 2], right[rows // 2 :])
    for s in range(right_ref.shape[0]):
        right_ref[s] = packed


def update_kernel(
    pair_ref, left_ref, right_ref, w_diff_ref, bias_ref, w_prod_ref, w_up_ref, w_down_ref, out_ref,
    rights, base, diffs,
):
    step = pl.program_id(0)
    lanes = pair_ref.shape[2]

    @pl.when(step == 0)
    def _():
        w_diff = w_diff_ref[...]
        half = right_ref.shape[1]
        first = lax.broadcasted_iota(jnp.int32, (half, lanes), 1) < lanes // 2
        for block in range(right_ref.shape[0]):
            packed = right_ref[block]
            swapped = pltpu.roll(packed, lanes // 2, 1)
            start = 2 * half * block
            rights[start : start + half, :] = jnp.where(first, packed, swapped)
            rights[start + half : start + 2 * half, :] = jnp.where(first, swapped, packed)
        base[...] = bias_ref[...] - dot(rights[:, : lanes // 2], w_diff)
        diffs[...] = dot(left_ref[:, : lanes // 2], w_diff)

    first = lax.broadcasted_iota(jnp.int32, base.shape, 1) < lanes // 2
    for r in range(ROWS_PER_STEP):
        i = step * ROWS_PER_STEP + r
        product = rights[...] * left_ref[pl.ds(i, 1), :]
        high = product.astype(BF).astype(F32)
        both = jnp.where(first, high, product - high).astype(BF)
        mid = (
            pair_ref[r]
            + bdot(jnp.concatenate([both, both], axis=1), w_prod_ref[...])
            + (base[...] + diffs[pl.ds(i, 1), :])
        )
        n_high, n_low = ksplit(channel_norm(mid))
        up = bdot(jnp.concatenate([n_high, n_low, n_high, n_low], axis=1), w_up_ref[...])
        h_high, h_low = ksplit(jnp.maximum(up, 0.0))
        down = bdot(jnp.concatenate([h_high, h_low], axis=1), w_down_ref[...])
        out_ref[r] = mid + (down[:, :lanes] + down[:, lanes:])


def update_pair(pair, left, right, w_outer, outer_bias, w_up, w_down):
    rows, cols, channels = pair.shape
    proj = w_outer.shape[0] // 2
    hidden = w_up.shape[1]
    p_high, p_low = split(w_outer[:proj])
    u_high, u_low = split(w_up)
    d_high, d_low = split(w_down)
    w_prod = jnp.concatenate([p_high, p_high, p_low, p_low], axis=0)
    w_up4 = jnp.concatenate([u_high, u_high, u_low, u_low], axis=0)
    d_both = jnp.concatenate([d_high, d_low], axis=1)
    w_down4 = jnp.concatenate([d_both, d_both], axis=0)
    whole = lambda x: pl.BlockSpec(x.shape, lambda s: (0,) * x.ndim)
    block = pl.BlockSpec((ROWS_PER_STEP, cols, channels), lambda s: (s, 0, 0))
    fixed = (left, right, w_outer[proj:], outer_bias[None, :], w_prod, w_up4, w_down4)
    cells = rows * cols
    return pl.pallas_call(
        update_kernel,
        grid=(rows // ROWS_PER_STEP,),
        in_specs=[block] + [whole(x) for x in fixed],
        out_specs=block,
        out_shape=jax.ShapeDtypeStruct(pair.shape, F32),
        scratch_shapes=[
            pltpu.VMEM((cols, channels), F32),
            pltpu.VMEM((cols, channels), F32),
            pltpu.VMEM((rows, channels), F32),
        ],
        compiler_params=pltpu.CompilerParams(vmem_limit_bytes=40 * 2**20),
        cost_estimate=pl.CostEstimate(
            flops=2 * cells * channels * (4 * hidden + 4 * hidden + 256),
            bytes_accessed=8 * cells * channels,
            transcendentals=cells,
        ),
        name="update_pair",
    )(pair, *fixed)


def spread_to(x, axis):
    return lax.all_to_all(jnp.broadcast_to(x, (lax.axis_size(axis),) + x.shape), axis, 0, 0)


def per_device(
    seq, query, key, value, pair, w_bias, w_out, w_left, w_right, w_outer, outer_bias, w_up, w_down
):
    rows, cols, channels = pair.shape
    heads = w_bias.shape[1]
    width = w_out.shape[0]
    head_dim = width // heads
    n_row, n_col = lax.axis_size("row"), lax.axis_size("col")
    group = heads // n_col
    scale = 1.0 / jnp.sqrt(jnp.float32(head_dim))

    half = cols // 2
    own = jnp.concatenate([key[:half], value[:half], key[half:], value[half:]], axis=1)
    pairs = [[z * 2 + k for z in range(n_row // 2)] for k in range(2)]
    across = lax.all_to_all(
        jnp.broadcast_to(own, (n_row // 2,) + own.shape), "row", 0, 0, axis_index_groups=pairs
    )
    other = lax.ppermute(across, "row", [(i, i ^ 1) for i in range(n_row)])
    even = (lax.axis_index("row") % 2 == 0)
    kv = jnp.where(even, jnp.stack([across, other], 1), jnp.stack([other, across], 1))
    kv = kv.reshape(heads, half, 2, 2, head_dim).transpose(3, 0, 2, 1, 4)
    keys = kv[0].reshape(heads, cols, head_dim)
    values = kv[1].reshape(heads, cols, head_dim)
    queries = spread_to(query, "col").reshape(n_col, rows, group, head_dim)
    queries = queries.transpose(0, 2, 1, 3).reshape(heads, rows, head_dim)

    bias = jnp.einsum("ijc,ch->hij", channel_norm(pair), w_bias, precision=HIGH)
    scores = jnp.einsum("hid,hjd->hij", queries, keys, precision=HIGH) * scale + bias
    top = jnp.max(scores, axis=2)
    expo = jnp.exp(scores - top[..., None])
    totals = jnp.sum(expo, axis=2)
    weighted = jnp.einsum("hij,hjd->hid", expo, values, precision=HIGH)

    stats = jnp.concatenate([top.reshape(n_col, group, rows), totals.reshape(n_col, group, rows)], axis=1)
    stats = jnp.pad(stats, ((0, 0), (0, 0), (0, channels - rows)))
    shares = weighted.reshape(n_col, group, rows, head_dim).transpose(0, 2, 1, 3).reshape(n_col, rows, channels)
    parts = lax.all_to_all(jnp.concatenate([shares, stats], axis=1), "col", 0, 0)

    attn = pl.pallas_call(
        functools.partial(merge_kernel, group),
        out_shape=jax.ShapeDtypeStruct((n_col, rows, channels), F32),
        name="merge",
    )(parts)
    attn = lax.all_to_all(attn, "col", 0, 0)
    seq_new, shares = pl.pallas_call(
        project_kernel,
        out_shape=(
            jax.ShapeDtypeStruct(seq.shape, F32),
            jax.ShapeDtypeStruct((n_col, rows + 8, channels), F32),
        ),
        name="project",
    )(attn, w_out, seq, jnp.concatenate([w_left, w_right], axis=1))
    shares = lax.all_to_all(shares, "col", 0, 0)
    left, right = pl.pallas_call(
        functools.partial(left_right_kernel, width),
        out_shape=(
            jax.ShapeDtypeStruct((rows, channels), F32),
            jax.ShapeDtypeStruct((n_row, rows // 2, channels), F32),
        ),
        name="left_right",
    )(shares)
    every = lax.all_to_all(right, "row", 0, 0)
    blocks = cols // rows
    mine = lax.dynamic_slice_in_dim(every, lax.axis_index("col") * blocks, blocks, 0)
    return seq_new, update_pair(pair, left, mine, w_outer, outer_bias, w_up, w_down)


def solution(mesh):
    in_specs = (
        P("row", "col"),
        P("row", "col"),
        P("col", "row"),
        P("col", "row"),
        P("row", "col", None),
        P(),
        P(None, "col"),
        P("col", None),
        P("col", None),
        P(),
        P(),
        P(),
        P(),
    )
    out_specs = (P("row", "col"), P("row", "col", None))
    return jax.shard_map(
        per_device, mesh=mesh, in_specs=in_specs, out_specs=out_specs, check_vma=False
    )
```

```python
import functools

import jax
import jax.numpy as jnp
from jax import lax
from jax.experimental import pallas as pl
from jax.experimental.pallas import tpu as pltpu
from jax.sharding import PartitionSpec as P

HIGH = lax.Precision.HIGHEST
EPS = 1e-05
BF = jnp.bfloat16
F32 = jnp.float32
BIAS_ROWS = 16
ATTENTION_GROUPS = 4
UPDATE_ROWS = 24
CHUNK_ROWS = 4
MIB = 2**20


def dot(a, b, dims=((1,), (0,)), precision=HIGH):
    return lax.dot_general(a, b, (dims, ((), ())), precision=precision, preferred_element_type=F32)


def bdot(a, b, dims=((1,), (0,))):
    return lax.dot_general(a, b, (dims, ((), ())), preferred_element_type=F32)


def channel_norm(x):
    centre = x - jnp.mean(x, axis=-1, keepdims=True)
    return centre * lax.rsqrt(jnp.mean(centre * centre, axis=-1, keepdims=True) + EPS)


def split(x):
    high = lax.reduce_precision(x, 8, 7)
    return high.astype(BF), (x - high).astype(BF)


def ksplit(x):
    high = x.astype(BF)
    return high, (x - high.astype(F32)).astype(BF)


def merge_kernel(group, parts_ref, out_ref):
    sources, _, lanes = parts_ref.shape
    rows = out_ref.shape[1]
    tops = [parts_ref[s, rows : rows + group, :] for s in range(sources)]
    top = functools.reduce(jnp.maximum, tops)
    scales = [jnp.exp(t - top) for t in tops]
    total = sum(parts_ref[s, rows + group :, :] * scales[s] for s in range(sources))
    factors = jnp.concatenate([x / total for x in scales], axis=0)
    factors = jnp.concatenate([factors, jnp.zeros((lanes - sources * group, lanes), F32)], axis=0)
    factors = jnp.transpose(factors)[:rows]
    head = lax.broadcasted_iota(jnp.int32, (rows, lanes), 1) // (lanes // group)
    attn = jnp.zeros((rows, lanes), F32)
    for s in range(sources):
        factor = factors[:, s * group : s * group + 1]
        for h in range(1, group):
            factor = jnp.where(head == h, factors[:, s * group + h : s * group + h + 1], factor)
        attn = attn + parts_ref[s, :rows, :] * factor
    for s in range(sources):
        out_ref[s] = attn


def project_kernel(attn_ref, w_out_ref, seq_ref, w_lr_ref, seq_new_ref, out_ref):
    sources, rows, lanes = attn_ref.shape
    attn = jnp.concatenate([attn_ref[s] for s in range(sources)], axis=1)
    both = bdot(jnp.concatenate(ksplit(attn), axis=0), w_out_ref[...])
    both = both[:, :lanes] + both[:, lanes:]
    total = seq_ref[...] + (both[:rows] + both[rows:])
    seq_new_ref[...] = total
    w_lr = w_lr_ref[...]
    part = dot(total, w_lr)
    ones = jnp.ones((8, lanes), F32)
    sums = dot(ones, total, ((1,), (1,)))
    squares = dot(ones, total * total, ((1,), (1,)))
    row = lax.broadcasted_iota(jnp.int32, (8, rows), 0)
    stats = jnp.where(row == 0, sums, squares)
    columns = jnp.sum(w_lr, axis=0, keepdims=True)
    for s in range(out_ref.shape[0]):
        out_ref[s, :rows, :] = part
        out_ref[s, rows : rows + 8, :] = jnp.zeros((8, lanes), F32)
        out_ref[s, rows : rows + 2, :rows] = stats[:2]
        out_ref[s, rows + 2 : rows + 3, :] = columns


def left_right_kernel(width, parts_ref, left_ref, right_ref):
    sources = parts_ref.shape[0]
    rows, lanes = left_ref.shape
    total = parts_ref[0]
    for s in range(1, sources):
        total = total + parts_ref[s]
    stats = jnp.transpose(total[rows : rows + 8, :])
    mean = stats[:rows, 0:1] / width
    square = stats[:rows, 1:2] / width
    both = (total[:rows] - mean * total[rows + 2 : rows + 3]) * lax.rsqrt(square - mean * mean + EPS)
    swapped = pltpu.roll(both, lanes // 2, 1)
    first = lax.broadcasted_iota(jnp.int32, (rows, lanes), 1) < lanes // 2
    left_ref[...] = jnp.where(first, both, swapped)
    right = jnp.where(first, swapped, both)
    packed = jnp.where(first[: rows // 2], right[: rows // 2], right[rows // 2 :])
    for s in range(right_ref.shape[0]):
        right_ref[s] = packed


def pack_kernel(key_ref, value_ref, kv_ref):
    lanes = kv_ref.shape[2]
    tails = jnp.concatenate([key_ref[:, lanes:], value_ref[:, lanes:]], axis=1)
    packed = jnp.concatenate([key_ref[:, :lanes], value_ref[:, :lanes], tails], axis=0)
    for s in range(kv_ref.shape[0]):
        kv_ref[s] = packed


def bias_kernel(pair_ref, w_ref, out_ref):
    heads, steps, _ = out_ref.shape
    for r in range(steps):
        high, low = ksplit(channel_norm(pair_ref[r]))
        both = bdot(w_ref[...], jnp.concatenate([high, low], axis=1), ((1,), (1,)))
        out_ref[:, r, :] = both[:heads] + both[heads:]


def pair_bias(pair, w_bias):
    rows, cols, channels = pair.shape
    heads = w_bias.shape[1]
    high, low = split(w_bias.T)
    w = jnp.concatenate([jnp.concatenate([x, x], axis=1) for x in (high, low)], axis=0)
    block = pl.BlockSpec((BIAS_ROWS, cols, channels), lambda s: (s, 0, 0))
    return pl.pallas_call(
        bias_kernel,
        grid=(rows // BIAS_ROWS,),
        in_specs=[
            block,
            pl.BlockSpec(w.shape, lambda s: (0, 0)),
        ],
        out_specs=pl.BlockSpec((heads, BIAS_ROWS, cols), lambda s: (0, s, 0)),
        out_shape=jax.ShapeDtypeStruct((heads, rows, cols), F32),
        compiler_params=pltpu.CompilerParams(vmem_limit_bytes=24 * MIB),
        cost_estimate=pl.CostEstimate(
            flops=12 * rows * cols * channels * heads,
            bytes_accessed=4 * rows * cols * (channels + heads),
            transcendentals=rows * cols,
        ),
        name="pair_bias",
    )(pair, w)


def attention_kernel(place_ref, q_ref, own_ref, other_ref, bias_ref, out_ref):
    rows, lanes = q_ref.shape[1:]
    cols = bias_ref.shape[2]
    steps = out_ref.shape[0]
    group = bias_ref.shape[0] // steps
    hd = lanes // group
    even = place_ref[0] == 0
    scale = 1.0 / hd**0.5
    lane = lax.broadcasted_iota(jnp.int32, (rows, lanes), 1)
    for g in range(steps):
        heads = []
        for p in range(g * group // 2, (g + 1) * group // 2):
            own, other = own_ref[p], other_ref[p]
            heads += [jnp.where(even, own, other), jnp.where(even, other, own)]
        tails = jnp.concatenate([x[2 * hd :] for x in heads], axis=0)
        keys = jnp.concatenate([x[:hd] for x in heads], axis=0)
        keys = jnp.concatenate([keys, tails[:, : lanes // 2]], axis=1)
        values = jnp.concatenate([x[hd : 2 * hd] for x in heads], axis=0)
        values = jnp.concatenate([values, tails[:, lanes // 2 :]], axis=1)
        k_high, k_low = ksplit(keys)
        v_high, v_low = ksplit(values)
        q = q_ref[(pl.program_id(0) * steps + g) ^ place_ref[1]] * scale
        q = jnp.concatenate([jnp.where(lane // hd == h, q, 0.0) for h in range(group)], axis=0)
        q = jnp.concatenate(ksplit(q), axis=1)
        scores = bdot(q, jnp.concatenate([k_high, k_high], axis=0)) + bdot(q, jnp.concatenate([k_low, k_low], axis=0))
        scores = scores + bias_ref[g * group : (g + 1) * group].reshape(group * rows, cols)
        top = jnp.max(scores, axis=1, keepdims=True)
        expo = jnp.exp(scores - top)
        total = jnp.sum(expo, axis=1, keepdims=True)
        w = bdot(
            jnp.concatenate(ksplit(expo), axis=0), jnp.concatenate([v_high, v_low], axis=0), ((1,), (1,))
        )
        half = group * rows
        w = (w[:half, :lanes] + w[:half, lanes:]) + (w[half:, :lanes] + w[half:, lanes:])
        weighted = jnp.zeros((rows, lanes), F32)
        stats = jnp.zeros((rows, lanes), F32)
        for h in range(group):
            part = slice(h * rows, (h + 1) * rows)
            weighted = jnp.where(lane // hd == h, w[part], weighted)
            stats = jnp.where(lane == h, top[part], stats)
            stats = jnp.where(lane == h + group, total[part], stats)
        out_ref[g, :rows, :] = weighted
        stats = jnp.concatenate([stats, jnp.zeros((lanes - rows, lanes), F32)], axis=0)
        out_ref[g, rows:, :] = jnp.transpose(stats)[: 2 * group]


def attention(place, queries, own, other, bias):
    n_col, rows, lanes = queries.shape
    heads, _, cols = bias.shape
    group = heads // n_col
    steps = ATTENTION_GROUPS
    kv_block = pl.BlockSpec((steps * group // 2,) + own.shape[1:], lambda s: (s, 0, 0))
    return pl.pallas_call(
        attention_kernel,
        grid=(n_col // steps,),
        in_specs=[
            pl.BlockSpec(memory_space=pltpu.SMEM),
            pl.BlockSpec(queries.shape, lambda s: (0, 0, 0)),
            kv_block,
            kv_block,
            pl.BlockSpec((steps * group, rows, cols), lambda s: (s, 0, 0)),
        ],
        out_specs=pl.BlockSpec((steps, rows + 2 * group, lanes), lambda s: (s, 0, 0)),
        out_shape=jax.ShapeDtypeStruct((n_col, rows + 2 * group, lanes), F32),
        compiler_params=pltpu.CompilerParams(vmem_limit_bytes=24 * MIB),
        name="attention",
    )(place, queries, own, other, bias)


def update_kernel(
    place_ref, pair_ref, left_ref, own_ref, other_ref, w_diff_ref, bias_ref, w_prod_ref, w_up_ref, w_down_ref, out_ref,
    rights, base, diffs,
):
    step = pl.program_id(0)
    steps, _, lanes = pair_ref.shape

    @pl.when(step == 0)
    def _():
        w_diff = w_diff_ref[...]
        half = own_ref.shape[1]
        first = lax.broadcasted_iota(jnp.int32, (half, lanes), 1) < lanes // 2
        even = place_ref[0] == 0
        blocks = []
        for p in range(rights.shape[0] // (4 * half)):
            p = place_ref[1] * (rights.shape[0] // (4 * half)) + p
            own, other = own_ref[p], other_ref[p]
            blocks += [jnp.where(even, own, other), jnp.where(even, other, own)]
        for block, packed in enumerate(blocks):
            swapped = pltpu.roll(packed, lanes // 2, 1)
            start = 2 * half * block
            rights[start : start + half, :] = jnp.where(first, packed, swapped)
            rights[start + half : start + 2 * half, :] = jnp.where(first, swapped, packed)
        base[...] = bias_ref[...] - dot(rights[:, : lanes // 2], w_diff)
        diffs[...] = dot(left_ref[:, : lanes // 2], w_diff)

    first = lax.broadcasted_iota(jnp.int32, base.shape, 1) < lanes // 2

    def normalize(start):
        products, mid = [], []
        for r in range(start, start + CHUNK_ROWS):
            i = step * steps + r
            product = rights[...] * left_ref[pl.ds(i, 1), :]
            high = product.astype(BF).astype(F32)
            products.append(jnp.where(first, high, product - high).astype(BF))
            mid.append(pair_ref[r] + (base[...] + diffs[pl.ds(i, 1), :]))
        products = jnp.concatenate(products, axis=0)
        mid = jnp.concatenate(mid, axis=0) + bdot(jnp.concatenate([products, products], axis=1), w_prod_ref[...])
        high, low = ksplit(channel_norm(mid))
        return mid, jnp.concatenate([high, low, high, low], axis=1)

    def transition(start, mid, normed):
        hidden = ksplit(jnp.maximum(bdot(normed, w_up_ref[...]), 0.0))
        down = bdot(jnp.concatenate(hidden, axis=1), w_down_ref[...])
        out = mid + (down[:, :lanes] + down[:, lanes:])
        out_ref[start : start + CHUNK_ROWS] = out.reshape((CHUNK_ROWS,) + out_ref.shape[1:])

    current = normalize(0)
    for start in range(0, steps, CHUNK_ROWS):
        following = normalize(start + CHUNK_ROWS) if start + CHUNK_ROWS < steps else None
        transition(start, *current)
        current = following


def update_weights(w_outer, w_up, w_down):
    p_high, p_low = split(w_outer[: w_outer.shape[0] // 2])
    u_high, u_low = split(w_up)
    down = jnp.concatenate(split(w_down), axis=1)
    return (
        jnp.concatenate([p_high, p_high, p_low, p_low], axis=0),
        jnp.concatenate([u_high, u_high, u_low, u_low], axis=0),
        jnp.concatenate([down, down], axis=0),
    )


def update_pair(place, pair, left, rights, w_diff, outer_bias, w_prod, w_up, w_down):
    rows, cols, channels = pair.shape
    hidden = w_up.shape[1]
    whole = lambda x: pl.BlockSpec(x.shape, lambda s: (0,) * x.ndim)
    block = pl.BlockSpec((UPDATE_ROWS, cols, channels), lambda s: (s, 0, 0))
    fixed = (left, *rights, w_diff, outer_bias[None, :], w_prod, w_up, w_down)
    cells = rows * cols
    return pl.pallas_call(
        update_kernel,
        grid=(rows // UPDATE_ROWS,),
        in_specs=[pl.BlockSpec(memory_space=pltpu.SMEM), block] + [whole(x) for x in fixed],
        out_specs=block,
        out_shape=jax.ShapeDtypeStruct(pair.shape, F32),
        scratch_shapes=[
            pltpu.VMEM((cols, channels), F32),
            pltpu.VMEM((cols, channels), F32),
            pltpu.VMEM((rows, channels), F32),
        ],
        compiler_params=pltpu.CompilerParams(vmem_limit_bytes=50 * MIB),
        cost_estimate=pl.CostEstimate(
            flops=2 * cells * channels * (8 * hidden + 256),
            bytes_accessed=8 * cells * channels,
            transcendentals=cells,
        ),
        name="update_pair",
    )(place, pair, *fixed)


def after(x, *others):
    place = pl.BlockSpec(memory_space=pl.ANY)
    return pl.pallas_call(
        lambda *refs: None,
        in_specs=[place] * (1 + len(others)),
        out_specs=place,
        out_shape=jax.ShapeDtypeStruct(x.shape, x.dtype),
        input_output_aliases={0: 0},
        compiler_params=pltpu.CompilerParams(vmem_limit_bytes=MIB),
        name="after",
    )(x, *others)


def per_device(
    seq, query, key, value, pair, w_bias, w_out, w_left, w_right, w_outer, outer_bias, w_up, w_down
):
    rows, cols, channels = pair.shape
    heads = w_bias.shape[1]
    width = w_out.shape[0]
    head_dim = width // heads
    n_row, n_col = lax.axis_size("row"), lax.axis_size("col")
    group = heads // n_col

    kv = pl.pallas_call(
        pack_kernel,
        out_shape=jax.ShapeDtypeStruct((n_row // 2, 3 * head_dim, channels), F32),
        name="pack",
    )(key.T, value.T)
    queries = query[None]
    hop = 1
    while hop < n_col:
        other = lax.ppermute(queries, "col", [(i, i ^ hop) for i in range(n_col)])
        queries = jnp.concatenate([queries, other], axis=0)
        hop *= 2
    pairs = [[z * 2 + k for z in range(n_row // 2)] for k in range(2)]
    own = lax.all_to_all(kv, "row", 0, 0, axis_index_groups=pairs)
    bias = pair_bias(pair, w_bias)
    weights = update_weights(w_outer, w_up, w_down)
    w_out = jnp.concatenate(split(w_out), axis=1)
    w_lr = jnp.concatenate([w_left, w_right], axis=1)
    own = after(own, queries, bias, w_out, w_lr, *weights)
    across = [(i, i ^ 1) for i in range(n_row)]
    other = lax.ppermute(own, "row", across)
    place = jnp.stack([lax.axis_index("row") % 2, lax.axis_index("col")])
    parts = attention(place, queries, own, other, bias)
    parts = lax.all_to_all(parts, "col", 0, 0)

    attn = pl.pallas_call(
        functools.partial(merge_kernel, group),
        out_shape=jax.ShapeDtypeStruct((n_col, rows, channels), F32),
        compiler_params=pltpu.CompilerParams(vmem_limit_bytes=8 * MIB),
        name="merge",
    )(parts)
    attn = lax.all_to_all(attn, "col", 0, 0)
    seq_new, shares = pl.pallas_call(
        project_kernel,
        out_shape=(
            jax.ShapeDtypeStruct(seq.shape, F32),
            jax.ShapeDtypeStruct((n_col, rows + 8, channels), F32),
        ),
        compiler_params=pltpu.CompilerParams(vmem_limit_bytes=8 * MIB),
        name="project",
    )(attn, w_out, seq, w_lr)
    shares = lax.all_to_all(shares, "col", 0, 0)
    left, right = pl.pallas_call(
        functools.partial(left_right_kernel, width),
        out_shape=(
            jax.ShapeDtypeStruct((rows, channels), F32),
            jax.ShapeDtypeStruct((n_row // 2, rows // 2, channels), F32),
        ),
        compiler_params=pltpu.CompilerParams(vmem_limit_bytes=8 * MIB),
        name="left_right",
    )(shares)
    right = lax.all_to_all(right, "row", 0, 0, axis_index_groups=pairs)
    rights = (right, lax.ppermute(right, "row", across))
    return seq_new, update_pair(place, pair, left, rights, w_outer[w_outer.shape[0] // 2 :], outer_bias, *weights)


def solution(mesh):
    in_specs = (
        P("row", "col"),
        P("row", "col"),
        P("col", "row"),
        P("col", "row"),
        P("row", "col", None),
        P(),
        P(None, "col"),
        P("col", None),
        P("col", None),
        P(),
        P(),
        P(),
        P(),
    )
    out_specs = (P("row", "col"), P("row", "col", None))
    return jax.shard_map(
        per_device, mesh=mesh, in_specs=in_specs, out_specs=out_specs, check_vma=False
    )
```

```python
import functools

import jax
import jax.numpy as jnp
from jax import lax
from jax.experimental import pallas as pl
from jax.experimental.pallas import tpu as pltpu
from jax.sharding import PartitionSpec as P

HIGH = lax.Precision.HIGHEST
EPS = 1e-05
BF = jnp.bfloat16
F32 = jnp.float32
BIAS_ROWS = 16
UPDATE_ROWS = 24
CHUNK_ROWS = 4
MIB = 2**20
HOPS = (
    ((2, 1), (3, 1), (3, 0), (0, 1), (0, 0), (1, 0), (1, 1), (2, 0)),
    ((2, 0), (1, 0), (3, 1), (0, 0), (0, 1), (1, 1), (2, 1), (3, 0)),
)


def dot(a, b, dims=((1,), (0,)), precision=HIGH):
    return lax.dot_general(a, b, (dims, ((), ())), precision=precision, preferred_element_type=F32)


def bdot(a, b, dims=((1,), (0,))):
    return lax.dot_general(a, b, (dims, ((), ())), preferred_element_type=F32)


def channel_norm(x):
    centre = x - jnp.mean(x, axis=-1, keepdims=True)
    return centre * lax.rsqrt(jnp.mean(centre * centre, axis=-1, keepdims=True) + EPS)


def ksplit(x):
    high = x.astype(BF)
    return high, (x - high.astype(F32)).astype(BF)


def merge_kernel(group, parts_ref, out_ref):
    sources, _, lanes = parts_ref.shape
    rows = out_ref.shape[1]
    tops = [parts_ref[s, rows : rows + group, :] for s in range(sources)]
    top = functools.reduce(jnp.maximum, tops)
    scales = [jnp.exp(t - top) for t in tops]
    total = sum(parts_ref[s, rows + group :, :] * scales[s] for s in range(sources))
    factors = jnp.concatenate([x / total for x in scales], axis=0)
    factors = jnp.concatenate([factors, jnp.zeros((lanes - sources * group, lanes), F32)], axis=0)
    factors = jnp.transpose(factors)[:rows]
    head = lax.broadcasted_iota(jnp.int32, (rows, lanes), 1) // (lanes // group)
    attn = jnp.zeros((rows, lanes), F32)
    for s in range(sources):
        factor = factors[:, s * group : s * group + 1]
        for h in range(1, group):
            factor = jnp.where(head == h, factors[:, s * group + h : s * group + h + 1], factor)
        attn = attn + parts_ref[s, :rows, :] * factor
    for s in range(sources):
        out_ref[s] = attn


def project_kernel(attn_ref, w_out_ref, seq_ref, w_left_ref, w_right_ref, seq_new_ref, out_ref):
    sources, rows, lanes = attn_ref.shape
    attn = jnp.concatenate([attn_ref[s] for s in range(sources)], axis=1)
    both = bdot(jnp.concatenate(ksplit(attn), axis=0), jnp.concatenate(ksplit(w_out_ref[...]), axis=1))
    both = both[:, :lanes] + both[:, lanes:]
    total = seq_ref[...] + (both[:rows] + both[rows:])
    seq_new_ref[...] = total
    w_lr = jnp.concatenate([w_left_ref[...], w_right_ref[...]], axis=0)
    part = dot(total, w_lr, ((1,), (1,)))
    ones = jnp.ones((8, lanes), F32)
    sums = dot(ones, total, ((1,), (1,)))
    squares = dot(ones, total * total, ((1,), (1,)))
    row = lax.broadcasted_iota(jnp.int32, (8, rows), 0)
    stats = jnp.where(row == 0, sums, squares)
    columns = dot(ones, w_lr, ((1,), (1,)))[:1]
    for s in range(out_ref.shape[0]):
        out_ref[s, :rows, :] = part
        out_ref[s, rows : rows + 8, :] = jnp.zeros((8, lanes), F32)
        out_ref[s, rows : rows + 2, :rows] = stats[:2]
        out_ref[s, rows + 2 : rows + 3, :] = columns


def left_right_kernel(width, parts_ref, left_ref, right_ref):
    sources = parts_ref.shape[0]
    rows, lanes = left_ref.shape
    total = parts_ref[0]
    for s in range(1, sources):
        total = total + parts_ref[s]
    stats = jnp.transpose(total[rows : rows + 8, :])
    mean = stats[:rows, 0:1] / width
    square = stats[:rows, 1:2] / width
    both = (total[:rows] - mean * total[rows + 2 : rows + 3]) * lax.rsqrt(square - mean * mean + EPS)
    swapped = pltpu.roll(both, lanes // 2, 1)
    first = lax.broadcasted_iota(jnp.int32, (rows, lanes), 1) < lanes // 2
    left_ref[...] = jnp.where(first, both, swapped)
    right = jnp.where(first, swapped, both)
    right_ref[...] = jnp.where(first[: rows // 2], right[: rows // 2], right[rows // 2 :])


def pack_kernel(key_ref, value_ref, kv_ref):
    lanes = kv_ref.shape[2]
    tails = jnp.concatenate([key_ref[:, lanes:], value_ref[:, lanes:]], axis=1)
    packed = jnp.concatenate([key_ref[:, :lanes], value_ref[:, :lanes], tails], axis=0)
    for s in range(kv_ref.shape[0]):
        kv_ref[s] = packed


def bias_kernel(pair_ref, w_ref, out_ref, done_ref):
    heads, steps, _ = out_ref.shape
    done_ref[...] = jnp.zeros(done_ref.shape, F32)
    w = jnp.concatenate([jnp.concatenate([x, x], axis=1) for x in ksplit(w_ref[...])], axis=0)
    for r in range(steps):
        high, low = ksplit(channel_norm(pair_ref[r]))
        both = bdot(w, jnp.concatenate([high, low], axis=1), ((1,), (1,)))
        out_ref[:, r, :] = both[:heads] + both[heads:]


def pair_bias(pair, w_bias):
    rows, cols, channels = pair.shape
    heads = w_bias.shape[1]
    w = w_bias.T
    block = pl.BlockSpec((BIAS_ROWS, cols, channels), lambda s: (s, 0, 0))
    return pl.pallas_call(
        bias_kernel,
        grid=(rows // BIAS_ROWS,),
        in_specs=[
            block,
            pl.BlockSpec(w.shape, lambda s: (0, 0)),
        ],
        out_specs=(
            pl.BlockSpec((heads, BIAS_ROWS, cols), lambda s: (0, s, 0)),
            pl.BlockSpec((8, 128), lambda s: (0, 0)),
        ),
        out_shape=(jax.ShapeDtypeStruct((heads, rows, cols), F32), jax.ShapeDtypeStruct((8, 128), F32)),
        compiler_params=pltpu.CompilerParams(vmem_limit_bytes=24 * MIB),
        cost_estimate=pl.CostEstimate(
            flops=12 * rows * cols * channels * heads,
            bytes_accessed=4 * rows * cols * (channels + heads),
            transcendentals=rows * cols,
        ),
        name="pair_bias",
    )(pair, w)


def attention_kernel(place_ref, q_ref, far_ref, own_ref, other_ref, bias_ref, out_ref):
    rows, lanes = q_ref.shape[1:]
    cols = bias_ref.shape[2]
    steps = out_ref.shape[0]
    group = bias_ref.shape[0] // steps
    hd = lanes // group
    even = place_ref[0] == 0
    scale = 1.0 / hd**0.5
    lane = lax.broadcasted_iota(jnp.int32, (rows, lanes), 1)
    for g in range(steps):
        heads = []
        for p in range(g * group // 2, (g + 1) * group // 2):
            own, other = own_ref[p], other_ref[p]
            heads += [jnp.where(even, own, other), jnp.where(even, other, own)]
        tails = jnp.concatenate([x[2 * hd :] for x in heads], axis=0)
        keys = jnp.concatenate([x[:hd] for x in heads], axis=0)
        keys = jnp.concatenate([keys, tails[:, : lanes // 2]], axis=1)
        values = jnp.concatenate([x[hd : 2 * hd] for x in heads], axis=0)
        values = jnp.concatenate([values, tails[:, lanes // 2 :]], axis=1)
        k_high, k_low = ksplit(keys)
        v_high, v_low = ksplit(values)
        slot = g ^ place_ref[1]
        near = slot < q_ref.shape[0]
        slot = lax.rem(slot, q_ref.shape[0])
        q = jnp.where(near, q_ref[slot], far_ref[slot]) * scale
        q = jnp.concatenate([jnp.where(lane // hd == h, q, 0.0) for h in range(group)], axis=0)
        q = jnp.concatenate(ksplit(q), axis=1)
        scores = bdot(q, jnp.concatenate([k_high, k_high], axis=0)) + bdot(q, jnp.concatenate([k_low, k_low], axis=0))
        scores = scores + bias_ref[g * group : (g + 1) * group].reshape(group * rows, cols)
        top = jnp.max(scores, axis=1, keepdims=True)
        expo = jnp.exp(scores - top)
        total = jnp.sum(expo, axis=1, keepdims=True)
        w = bdot(
            jnp.concatenate(ksplit(expo), axis=0), jnp.concatenate([v_high, v_low], axis=0), ((1,), (1,))
        )
        half = group * rows
        w = (w[:half, :lanes] + w[:half, lanes:]) + (w[half:, :lanes] + w[half:, lanes:])
        weighted = jnp.zeros((rows, lanes), F32)
        stats = jnp.zeros((rows, lanes), F32)
        for h in range(group):
            part = slice(h * rows, (h + 1) * rows)
            weighted = jnp.where(lane // hd == h, w[part], weighted)
            stats = jnp.where(lane == h, top[part], stats)
            stats = jnp.where(lane == h + group, total[part], stats)
        out_ref[g, :rows, :] = weighted
        stats = jnp.concatenate([stats, jnp.zeros((lanes - rows, lanes), F32)], axis=0)
        out_ref[g, rows:, :] = jnp.transpose(stats)[: 2 * group]


def attention(place, queries, far_queries, own, other, bias):
    n_col, rows, lanes = 2 * queries.shape[0], *queries.shape[1:]
    heads, _, cols = bias.shape
    group = heads // n_col
    return pl.pallas_call(
        attention_kernel,
        in_specs=[pl.BlockSpec(memory_space=pltpu.SMEM)] + [pl.BlockSpec(memory_space=pltpu.VMEM)] * 5,
        out_shape=jax.ShapeDtypeStruct((n_col, rows + 2 * group, lanes), F32),
        compiler_params=pltpu.CompilerParams(vmem_limit_bytes=24 * MIB),
        name="attention",
    )(place, queries, far_queries, own, other, bias)


def update_kernel(
    place_ref, pair_ref, left_ref, own_ref, other_ref, w_outer_ref, bias_ref, w_up_ref, w_down_ref, out_ref,
    rights, base, diffs, w_prod, w_ups, w_downs,
):
    step = pl.program_id(0)
    steps, _, lanes = pair_ref.shape

    @pl.when(step == 0)
    def _():
        w_diff = w_outer_ref[lanes // 2 :, :]
        half = own_ref.shape[1]
        first = lax.broadcasted_iota(jnp.int32, (half, lanes), 1) < lanes // 2
        even = place_ref[0] == 0
        blocks = []
        for p in range(rights.shape[0] // (4 * half)):
            own, other = own_ref[p], other_ref[p]
            blocks += [jnp.where(even, own, other), jnp.where(even, other, own)]
        for block, packed in enumerate(blocks):
            swapped = pltpu.roll(packed, lanes // 2, 1)
            start = 2 * half * block
            rights[start : start + half, :] = jnp.where(first, packed, swapped)
            rights[start + half : start + 2 * half, :] = jnp.where(first, swapped, packed)
        base[...] = bias_ref[...] - dot(rights[:, : lanes // 2], w_diff)
        diffs[...] = dot(left_ref[:, : lanes // 2], w_diff)
        high, low = ksplit(w_outer_ref[: lanes // 2, :])
        w_prod[...] = jnp.concatenate([high, high, low, low], axis=0)
        high, low = ksplit(w_up_ref[...])
        w_ups[...] = jnp.concatenate([high, high, low, low], axis=0)
        both = jnp.concatenate(ksplit(w_down_ref[...]), axis=1)
        w_downs[...] = jnp.concatenate([both, both], axis=0)

    first = lax.broadcasted_iota(jnp.int32, base.shape, 1) < lanes // 2

    def normalize(start):
        products, mid = [], []
        for r in range(start, start + CHUNK_ROWS):
            i = step * steps + r
            product = rights[...] * left_ref[pl.ds(i, 1), :]
            high = product.astype(BF).astype(F32)
            products.append(jnp.where(first, high, product - high).astype(BF))
            mid.append(pair_ref[r] + (base[...] + diffs[pl.ds(i, 1), :]))
        products = jnp.concatenate(products, axis=0)
        mid = jnp.concatenate(mid, axis=0) + bdot(jnp.concatenate([products, products], axis=1), w_prod[...])
        high, low = ksplit(channel_norm(mid))
        return mid, jnp.concatenate([high, low, high, low], axis=1)

    def transition(start, mid, normed):
        hidden = ksplit(jnp.maximum(bdot(normed, w_ups[...]), 0.0))
        down = bdot(jnp.concatenate(hidden, axis=1), w_downs[...])
        out = mid + (down[:, :lanes] + down[:, lanes:])
        out_ref[start : start + CHUNK_ROWS] = out.reshape((CHUNK_ROWS,) + out_ref.shape[1:])

    current = normalize(0)
    for start in range(0, steps, CHUNK_ROWS):
        following = normalize(start + CHUNK_ROWS) if start + CHUNK_ROWS < steps else None
        transition(start, *current)
        current = following


def update_pair(place, pair, left, rights, w_outer, outer_bias, w_up, w_down):
    rows, cols, channels = pair.shape
    hidden = w_up.shape[1]
    whole = lambda x: pl.BlockSpec(x.shape, lambda s: (0,) * x.ndim)
    block = pl.BlockSpec((UPDATE_ROWS, cols, channels), lambda s: (s, 0, 0))
    fixed = (left, *rights, w_outer, outer_bias[None, :], w_up, w_down)
    cells = rows * cols
    return pl.pallas_call(
        update_kernel,
        grid=(rows // UPDATE_ROWS,),
        in_specs=[pl.BlockSpec(memory_space=pltpu.SMEM), block] + [whole(x) for x in fixed],
        out_specs=block,
        out_shape=jax.ShapeDtypeStruct(pair.shape, F32),
        scratch_shapes=[
            pltpu.VMEM((cols, channels), F32),
            pltpu.VMEM((cols, channels), F32),
            pltpu.VMEM((rows, channels), F32),
            pltpu.VMEM((2 * w_outer.shape[0], channels), BF),
            pltpu.VMEM((4 * channels, hidden), BF),
            pltpu.VMEM((2 * hidden, 2 * channels), BF),
        ],
        compiler_params=pltpu.CompilerParams(vmem_limit_bytes=50 * MIB),
        cost_estimate=pl.CostEstimate(
            flops=2 * cells * channels * (8 * hidden + 256),
            bytes_accessed=8 * cells * channels,
            transcendentals=cells,
        ),
        name="update_pair",
    )(place, pair, *fixed)


def after(x, *others):
    place = pl.BlockSpec(memory_space=pl.ANY)
    return pl.pallas_call(
        lambda *refs: None,
        in_specs=[place] * (1 + len(others)),
        out_specs=place,
        out_shape=jax.ShapeDtypeStruct(x.shape, x.dtype),
        input_output_aliases={0: 0},
        compiler_params=pltpu.CompilerParams(vmem_limit_bytes=MIB),
        name="after",
    )(x, *others)


def columns_first(n_row, n_col, other):
    pairs = []
    for k in range(n_col):
        for half in range(2):
            for core in range(2):
                for plane in range(n_row // 4):
                    x, y = HOPS[other][(plane - k) % (n_row // 4)]
                    source = ((k // 2 + x) % (n_col // 2)) * 2 + ((k % 2) ^ y)
                    pairs.append(
                        (((k * 2 + (half ^ other)) * 2 + core) * n_col + source, ((plane * 2 + half) * 2 + core) * n_col + k)
                    )
    return sorted(pairs)


def per_device(
    seq, query, key, value, pair, w_bias, w_out, w_left, w_right, w_outer, outer_bias, w_up, w_down
):
    rows, cols, channels = pair.shape
    heads = w_bias.shape[1]
    width = w_out.shape[0]
    head_dim = width // heads
    n_row, n_col = lax.axis_size("row"), lax.axis_size("col")
    group = heads // n_col

    kv = pl.pallas_call(
        pack_kernel,
        out_shape=jax.ShapeDtypeStruct((n_row // 2, 3 * head_dim, channels), F32),
        name="pack",
    )(key.T, value.T)
    queries = query[None]
    hop = 1
    while hop < n_col:
        if hop > 1:
            queries = jnp.concatenate([queries, far_queries], axis=0)
        far_queries = lax.ppermute(queries, "col", [(i, i ^ hop) for i in range(n_col)])
        hop *= 2
    pairs = [[z * 2 + k for z in range(n_row // 2)] for k in range(2)]
    own = lax.all_to_all(kv, "row", 0, 0, axis_index_groups=pairs)
    bias, bias_done = pair_bias(pair, w_bias)
    own = after(own, far_queries[:1, :8], bias_done)
    across = [(i, i ^ 1) for i in range(n_row)]
    other = lax.ppermute(own, "row", across)
    place = jnp.stack([lax.axis_index("row") % 2, lax.axis_index("col")])
    parts = attention(place, queries, far_queries, own, other, bias)
    parts = lax.all_to_all(parts, "col", 0, 0)

    attn = pl.pallas_call(
        functools.partial(merge_kernel, group),
        out_shape=jax.ShapeDtypeStruct((n_col, rows, channels), F32),
        compiler_params=pltpu.CompilerParams(vmem_limit_bytes=8 * MIB),
        name="merge",
    )(parts)
    attn = lax.all_to_all(attn, "col", 0, 0)
    seq_new, shares = pl.pallas_call(
        project_kernel,
        out_shape=(
            jax.ShapeDtypeStruct(seq.shape, F32),
            jax.ShapeDtypeStruct((n_col, rows + 8, channels), F32),
        ),
        compiler_params=pltpu.CompilerParams(vmem_limit_bytes=8 * MIB),
        name="project",
    )(attn, w_out, seq, w_left.T, w_right.T)
    shares = lax.all_to_all(shares, "col", 0, 0)
    left, right = pl.pallas_call(
        functools.partial(left_right_kernel, width),
        out_shape=(
            jax.ShapeDtypeStruct((rows, channels), F32),
            jax.ShapeDtypeStruct((rows // 2, channels), F32),
        ),
        compiler_params=pltpu.CompilerParams(vmem_limit_bytes=8 * MIB),
        name="left_right",
    )(shares)
    near, far = [lax.ppermute(right, ("row", "col"), columns_first(n_row, n_col, other)) for other in (0, 1)]
    second = lax.axis_index("row") // 2 % 2 == 1
    right = jnp.stack([jnp.where(second, far, near), jnp.where(second, near, far)])
    rights = (right, lax.ppermute(right, "row", across))
    return seq_new, update_pair(place, pair, left, rights, w_outer, outer_bias, w_up, w_down)


def solution(mesh):
    in_specs = (
        P("row", "col"),
        P("row", "col"),
        P("col", "row"),
        P("col", "row"),
        P("row", "col", None),
        P(),
        P(None, "col"),
        P("col", None),
        P("col", None),
        P(),
        P(),
        P(),
        P(),
    )
    out_specs = (P("row", "col"), P("row", "col", None))
    return jax.shard_map(
        per_device, mesh=mesh, in_specs=in_specs, out_specs=out_specs, check_vma=False
    )
```

```python
import functools

import jax
import jax.numpy as jnp
from jax import lax
from jax.experimental import pallas as pl
from jax.experimental.pallas import tpu as pltpu
from jax.sharding import PartitionSpec as P

HIGH = lax.Precision.HIGHEST
EPS = 1e-05
BF = jnp.bfloat16
F32 = jnp.float32
BIAS_ROWS = 16
UPDATE_ROWS = 24
CHUNK_ROWS = 4
MIB = 2**20
HOPS = (
    ((2, 1), (3, 1), (3, 0), (0, 1), (0, 0), (1, 0), (1, 1), (2, 0)),
    ((2, 0), (1, 0), (3, 1), (0, 0), (0, 1), (1, 1), (2, 1), (3, 0)),
)


def dot(a, b, dims=((1,), (0,)), precision=HIGH):
    return lax.dot_general(a, b, (dims, ((), ())), precision=precision, preferred_element_type=F32)


def bdot(a, b, dims=((1,), (0,))):
    return lax.dot_general(a, b, (dims, ((), ())), preferred_element_type=F32)


def channel_norm(x):
    centre = x - jnp.mean(x, axis=-1, keepdims=True)
    return centre * lax.rsqrt(jnp.mean(centre * centre, axis=-1, keepdims=True) + EPS)


def ksplit(x):
    high = x.astype(BF)
    return high, (x - high.astype(F32)).astype(BF)


def merge_kernel(group, parts_ref, out_ref):
    sources, _, lanes = parts_ref.shape
    rows = out_ref.shape[1]
    tops = [parts_ref[s, rows : rows + group, :] for s in range(sources)]
    top = functools.reduce(jnp.maximum, tops)
    scales = [jnp.exp(t - top) for t in tops]
    total = sum(parts_ref[s, rows + group :, :] * scales[s] for s in range(sources))
    factors = jnp.concatenate([x / total for x in scales], axis=0)
    factors = jnp.concatenate([factors, jnp.zeros((lanes - sources * group, lanes), F32)], axis=0)
    factors = jnp.transpose(factors)[:rows]
    head = lax.broadcasted_iota(jnp.int32, (rows, lanes), 1) // (lanes // group)
    attn = jnp.zeros((rows, lanes), F32)
    for s in range(sources):
        factor = factors[:, s * group : s * group + 1]
        for h in range(1, group):
            factor = jnp.where(head == h, factors[:, s * group + h : s * group + h + 1], factor)
        attn = attn + parts_ref[s, :rows, :] * factor
    for s in range(sources):
        out_ref[s] = attn


def project_kernel(attn_ref, w_out_ref, seq_ref, w_left_ref, w_right_ref, seq_new_ref, out_ref):
    sources, rows, lanes = attn_ref.shape
    attn = jnp.concatenate([attn_ref[s] for s in range(sources)], axis=1)
    both = bdot(jnp.concatenate(ksplit(attn), axis=0), jnp.concatenate(ksplit(w_out_ref[...]), axis=1))
    both = both[:, :lanes] + both[:, lanes:]
    total = seq_ref[...] + (both[:rows] + both[rows:])
    seq_new_ref[...] = total
    w_lr = jnp.concatenate([w_left_ref[...], w_right_ref[...]], axis=0)
    part = dot(total, w_lr, ((1,), (1,)))
    ones = jnp.ones((8, lanes), F32)
    sums = dot(ones, total, ((1,), (1,)))
    squares = dot(ones, total * total, ((1,), (1,)))
    row = lax.broadcasted_iota(jnp.int32, (8, rows), 0)
    stats = jnp.where(row == 0, sums, squares)
    columns = dot(ones, w_lr, ((1,), (1,)))[:1]
    for s in range(out_ref.shape[0]):
        out_ref[s, :rows, :] = part
        out_ref[s, rows : rows + 8, :] = jnp.zeros((8, lanes), F32)
        out_ref[s, rows : rows + 2, :rows] = stats[:2]
        out_ref[s, rows + 2 : rows + 3, :] = columns


def left_right_kernel(width, parts_ref, left_ref, right_ref):
    sources = parts_ref.shape[0]
    rows, lanes = left_ref.shape
    total = parts_ref[0]
    for s in range(1, sources):
        total = total + parts_ref[s]
    stats = jnp.transpose(total[rows : rows + 8, :])
    mean = stats[:rows, 0:1] / width
    square = stats[:rows, 1:2] / width
    both = (total[:rows] - mean * total[rows + 2 : rows + 3]) * lax.rsqrt(square - mean * mean + EPS)
    swapped = pltpu.roll(both, lanes // 2, 1)
    first = lax.broadcasted_iota(jnp.int32, (rows, lanes), 1) < lanes // 2
    left_ref[...] = jnp.where(first, both, swapped)
    right = jnp.where(first, swapped, both)
    right_ref[...] = jnp.where(first[: rows // 2], right[: rows // 2], right[rows // 2 :])


def pack_kernel(key_ref, value_ref, kv_ref):
    lanes = kv_ref.shape[2]
    tails = jnp.concatenate([key_ref[:, lanes:], value_ref[:, lanes:]], axis=1)
    packed = jnp.concatenate([key_ref[:, :lanes], value_ref[:, :lanes], tails], axis=0)
    for s in range(kv_ref.shape[0]):
        kv_ref[s] = packed


def bias_kernel(pair_ref, w_ref, out_ref, done_ref):
    heads, steps, _ = out_ref.shape
    done_ref[...] = jnp.zeros(done_ref.shape, F32)
    w = jnp.concatenate([jnp.concatenate([x, x], axis=1) for x in ksplit(w_ref[...])], axis=0)
    for r in range(steps):
        high, low = ksplit(channel_norm(pair_ref[r]))
        both = bdot(w, jnp.concatenate([high, low], axis=1), ((1,), (1,)))
        out_ref[:, r, :] = both[:heads] + both[heads:]


def pair_bias(pair, w_bias):
    rows, cols, channels = pair.shape
    heads = w_bias.shape[1]
    w = w_bias.T
    block = pl.BlockSpec((BIAS_ROWS, cols, channels), lambda s: (s, 0, 0))
    return pl.pallas_call(
        bias_kernel,
        grid=(rows // BIAS_ROWS,),
        in_specs=[
            block,
            pl.BlockSpec(w.shape, lambda s: (0, 0)),
        ],
        out_specs=(
            pl.BlockSpec((heads, BIAS_ROWS, cols), lambda s: (0, s, 0)),
            pl.BlockSpec((8, 128), lambda s: (0, 0)),
        ),
        out_shape=(jax.ShapeDtypeStruct((heads, rows, cols), F32), jax.ShapeDtypeStruct((8, 128), F32)),
        compiler_params=pltpu.CompilerParams(vmem_limit_bytes=24 * MIB),
        cost_estimate=pl.CostEstimate(
            flops=12 * rows * cols * channels * heads,
            bytes_accessed=4 * rows * cols * (channels + heads),
            transcendentals=rows * cols,
        ),
        name="pair_bias",
    )(pair, w)


def attention_kernel(place_ref, q_ref, far_ref, own_ref, other_ref, bias_ref, out_ref):
    rows, lanes = q_ref.shape[1:]
    cols = bias_ref.shape[2]
    steps = out_ref.shape[0]
    group = bias_ref.shape[0] // steps
    hd = lanes // group
    even = place_ref[0] == 0
    scale = 1.0 / hd**0.5
    lane = lax.broadcasted_iota(jnp.int32, (rows, lanes), 1)
    for g in range(steps):
        heads = []
        for p in range(g * group // 2, (g + 1) * group // 2):
            own, other = own_ref[p], other_ref[p]
            heads += [jnp.where(even, own, other), jnp.where(even, other, own)]
        tails = jnp.concatenate([x[2 * hd :] for x in heads], axis=0)
        keys = jnp.concatenate([x[:hd] for x in heads], axis=0)
        keys = jnp.concatenate([keys, tails[:, : lanes // 2]], axis=1)
        values = jnp.concatenate([x[hd : 2 * hd] for x in heads], axis=0)
        values = jnp.concatenate([values, tails[:, lanes // 2 :]], axis=1)
        k_high, k_low = ksplit(keys)
        v_high, v_low = ksplit(values)
        slot = g ^ place_ref[1]
        near = slot < q_ref.shape[0]
        slot = lax.rem(slot, q_ref.shape[0])
        q = jnp.where(near, q_ref[slot], far_ref[slot]) * scale
        q = jnp.concatenate([jnp.where(lane // hd == h, q, 0.0) for h in range(group)], axis=0)
        q = jnp.concatenate(ksplit(q), axis=1)
        scores = bdot(q, jnp.concatenate([k_high, k_high], axis=0)) + bdot(q, jnp.concatenate([k_low, k_low], axis=0))
        scores = scores + bias_ref[g * group : (g + 1) * group].reshape(group * rows, cols)
        top = jnp.max(scores, axis=1, keepdims=True)
        expo = jnp.exp(scores - top)
        total = jnp.sum(expo, axis=1, keepdims=True)
        w = bdot(
            jnp.concatenate(ksplit(expo), axis=0), jnp.concatenate([v_high, v_low], axis=0), ((1,), (1,))
        )
        half = group * rows
        w = (w[:half, :lanes] + w[:half, lanes:]) + (w[half:, :lanes] + w[half:, lanes:])
        weighted = jnp.zeros((rows, lanes), F32)
        stats = jnp.zeros((rows, lanes), F32)
        for h in range(group):
            part = slice(h * rows, (h + 1) * rows)
            weighted = jnp.where(lane // hd == h, w[part], weighted)
            stats = jnp.where(lane == h, top[part], stats)
            stats = jnp.where(lane == h + group, total[part], stats)
        out_ref[g, :rows, :] = weighted
        stats = jnp.concatenate([stats, jnp.zeros((lanes - rows, lanes), F32)], axis=0)
        out_ref[g, rows:, :] = jnp.transpose(stats)[: 2 * group]


def attention(place, queries, far_queries, own, other, bias):
    n_col, rows, lanes = 2 * queries.shape[0], *queries.shape[1:]
    heads, _, cols = bias.shape
    group = heads // n_col
    return pl.pallas_call(
        attention_kernel,
        in_specs=[pl.BlockSpec(memory_space=pltpu.SMEM)] + [pl.BlockSpec(memory_space=pltpu.VMEM)] * 5,
        out_shape=jax.ShapeDtypeStruct((n_col, rows + 2 * group, lanes), F32),
        compiler_params=pltpu.CompilerParams(vmem_limit_bytes=24 * MIB),
        name="attention",
    )(place, queries, far_queries, own, other, bias)


def update_kernel(
    place_ref, pair_ref, left_ref, own_ref, other_ref, w_outer_ref, bias_ref, w_up_ref, w_down_ref, out_ref,
    rights, base, diffs, w_prod, w_ups, w_downs,
):
    step = pl.program_id(0)
    steps, _, lanes = pair_ref.shape

    @pl.when(step == 0)
    def _():
        w_diff = w_outer_ref[lanes // 2 :, :]
        half = own_ref.shape[1]
        first = lax.broadcasted_iota(jnp.int32, (half, lanes), 1) < lanes // 2
        even = place_ref[0] == 0
        blocks = []
        for p in range(rights.shape[0] // (4 * half)):
            own, other = own_ref[p], other_ref[p]
            blocks += [jnp.where(even, own, other), jnp.where(even, other, own)]
        for block, packed in enumerate(blocks):
            swapped = pltpu.roll(packed, lanes // 2, 1)
            start = 2 * half * block
            rights[start : start + half, :] = jnp.where(first, packed, swapped)
            rights[start + half : start + 2 * half, :] = jnp.where(first, swapped, packed)
        base[...] = bias_ref[...] - dot(rights[:, : lanes // 2], w_diff)
        diffs[...] = dot(left_ref[:, : lanes // 2], w_diff)
        high, low = ksplit(w_outer_ref[: lanes // 2, :])
        w_prod[...] = jnp.concatenate([high, high, low, low], axis=0)
        high, low = ksplit(w_up_ref[...])
        w_ups[...] = jnp.concatenate([high, high, low, low], axis=0)
        both = jnp.concatenate(ksplit(w_down_ref[...]), axis=1)
        w_downs[...] = jnp.concatenate([both, both], axis=0)

    first = lax.broadcasted_iota(jnp.int32, base.shape, 1) < lanes // 2

    def normalize(start):
        products, mid = [], []
        for r in range(start, start + CHUNK_ROWS):
            i = step * steps + r
            product = rights[...] * left_ref[pl.ds(i, 1), :]
            high = product.astype(BF).astype(F32)
            products.append(jnp.where(first, high, product - high).astype(BF))
            mid.append(pair_ref[r] + (base[...] + diffs[pl.ds(i, 1), :]))
        products = jnp.concatenate(products, axis=0)
        mid = jnp.concatenate(mid, axis=0) + bdot(jnp.concatenate([products, products], axis=1), w_prod[...])
        high, low = ksplit(channel_norm(mid))
        return mid, jnp.concatenate([high, low, high, low], axis=1)

    def transition(start, mid, normed):
        hidden = ksplit(jnp.maximum(bdot(normed, w_ups[...]), 0.0))
        down = bdot(jnp.concatenate(hidden, axis=1), w_downs[...])
        out = mid + (down[:, :lanes] + down[:, lanes:])
        out_ref[start : start + CHUNK_ROWS] = out.reshape((CHUNK_ROWS,) + out_ref.shape[1:])

    current = normalize(0)
    for start in range(0, steps, CHUNK_ROWS):
        following = normalize(start + CHUNK_ROWS) if start + CHUNK_ROWS < steps else None
        transition(start, *current)
        current = following


def update_pair(place, pair, left, rights, w_outer, outer_bias, w_up, w_down):
    rows, cols, channels = pair.shape
    hidden = w_up.shape[1]
    whole = lambda x: pl.BlockSpec(x.shape, lambda s: (0,) * x.ndim)
    block = pl.BlockSpec((UPDATE_ROWS, cols, channels), lambda s: (s, 0, 0))
    fixed = (left, *rights, w_outer, outer_bias[None, :], w_up, w_down)
    cells = rows * cols
    return pl.pallas_call(
        update_kernel,
        grid=(rows // UPDATE_ROWS,),
        in_specs=[pl.BlockSpec(memory_space=pltpu.SMEM), block] + [whole(x) for x in fixed],
        out_specs=block,
        out_shape=jax.ShapeDtypeStruct(pair.shape, F32),
        scratch_shapes=[
            pltpu.VMEM((cols, channels), F32),
            pltpu.VMEM((cols, channels), F32),
            pltpu.VMEM((rows, channels), F32),
            pltpu.VMEM((2 * w_outer.shape[0], channels), BF),
            pltpu.VMEM((4 * channels, hidden), BF),
            pltpu.VMEM((2 * hidden, 2 * channels), BF),
        ],
        compiler_params=pltpu.CompilerParams(vmem_limit_bytes=57 * MIB),
        cost_estimate=pl.CostEstimate(
            flops=2 * cells * channels * (8 * hidden + 256),
            bytes_accessed=8 * cells * channels,
            transcendentals=cells,
        ),
        name="update_pair",
    )(place, pair, *fixed)


def after(x, *others):
    place = pl.BlockSpec(memory_space=pl.ANY)
    return pl.pallas_call(
        lambda *refs: None,
        in_specs=[place] * (1 + len(others)),
        out_specs=place,
        out_shape=jax.ShapeDtypeStruct(x.shape, x.dtype),
        input_output_aliases={0: 0},
        compiler_params=pltpu.CompilerParams(vmem_limit_bytes=MIB),
        name="after",
    )(x, *others)


def columns_first(n_row, n_col, other):
    pairs = []
    for k in range(n_col):
        for half in range(2):
            for core in range(2):
                for plane in range(n_row // 4):
                    x, y = HOPS[other][(plane - k) % (n_row // 4)]
                    source = ((k // 2 + x) % (n_col // 2)) * 2 + ((k % 2) ^ y)
                    pairs.append(
                        (((k * 2 + (half ^ other)) * 2 + core) * n_col + source, ((plane * 2 + half) * 2 + core) * n_col + k)
                    )
    return sorted(pairs)


def per_device(
    seq, query, key, value, pair, w_bias, w_out, w_left, w_right, w_outer, outer_bias, w_up, w_down
):
    rows, cols, channels = pair.shape
    heads = w_bias.shape[1]
    width = w_out.shape[0]
    head_dim = width // heads
    n_row, n_col = lax.axis_size("row"), lax.axis_size("col")
    group = heads // n_col

    kv = pl.pallas_call(
        pack_kernel,
        out_shape=jax.ShapeDtypeStruct((n_row // 2, 3 * head_dim, channels), F32),
        name="pack",
    )(key.T, value.T)
    queries = query[None]
    hop = 1
    while hop < n_col:
        if hop > 1:
            queries = jnp.concatenate([queries, far_queries], axis=0)
        far_queries = lax.ppermute(queries, "col", [(i, i ^ hop) for i in range(n_col)])
        hop *= 2
    pairs = [[z * 2 + k for z in range(n_row // 2)] for k in range(2)]
    own = lax.all_to_all(kv, "row", 0, 0, axis_index_groups=pairs)
    bias, bias_done = pair_bias(pair, w_bias)
    own = after(own, far_queries[:1, :8], bias_done)
    across = [(i, i ^ 1) for i in range(n_row)]
    other = lax.ppermute(own, "row", across)
    place = jnp.stack([lax.axis_index("row") % 2, lax.axis_index("col")])
    parts = attention(place, queries, far_queries, own, other, bias)
    parts = lax.all_to_all(parts, "col", 0, 0)

    attn = pl.pallas_call(
        functools.partial(merge_kernel, group),
        out_shape=jax.ShapeDtypeStruct((n_col, rows, channels), F32),
        compiler_params=pltpu.CompilerParams(vmem_limit_bytes=8 * MIB),
        name="merge",
    )(parts)
    attn = lax.all_to_all(attn, "col", 0, 0)
    seq_new, shares = pl.pallas_call(
        project_kernel,
        out_shape=(
            jax.ShapeDtypeStruct(seq.shape, F32),
            jax.ShapeDtypeStruct((n_col, rows + 8, channels), F32),
        ),
        compiler_params=pltpu.CompilerParams(vmem_limit_bytes=8 * MIB),
        name="project",
    )(attn, w_out, seq, w_left.T, w_right.T)
    shares = lax.all_to_all(shares, "col", 0, 0)
    left, right = pl.pallas_call(
        functools.partial(left_right_kernel, width),
        out_shape=(
            jax.ShapeDtypeStruct((rows, channels), F32),
            jax.ShapeDtypeStruct((rows // 2, channels), F32),
        ),
        compiler_params=pltpu.CompilerParams(vmem_limit_bytes=8 * MIB),
        name="left_right",
    )(shares)
    near, far = [lax.ppermute(right, ("row", "col"), columns_first(n_row, n_col, other)) for other in (0, 1)]
    second = lax.axis_index("row") // 2 % 2 == 1
    right = jnp.stack([jnp.where(second, far, near), jnp.where(second, near, far)])
    rights = (right, lax.ppermute(right, "row", across))
    return seq_new, update_pair(place, pair, left, rights, w_outer, outer_bias, w_up, w_down)


def solution(mesh):
    in_specs = (
        P("row", "col"),
        P("row", "col"),
        P("col", "row"),
        P("col", "row"),
        P("row", "col", None),
        P(),
        P(None, "col"),
        P("col", None),
        P("col", None),
        P(),
        P(),
        P(),
        P(),
    )
    out_specs = (P("row", "col"), P("row", "col", None))
    return jax.shard_map(
        per_device, mesh=mesh, in_specs=in_specs, out_specs=out_specs, check_vma=False
    )
```

```python
import functools

import jax
import jax.numpy as jnp
from jax import lax
from jax.experimental import pallas as pl
from jax.experimental.pallas import tpu as pltpu
from jax.sharding import PartitionSpec as P

HIGH = lax.Precision.HIGHEST
EPS = 1e-05
BF = jnp.bfloat16
F32 = jnp.float32
BIAS_ROWS = 16
CHUNK_ROWS = 4
MIB = 2**20
HOPS = (
    ((2, 1), (3, 1), (3, 0), (0, 1), (0, 0), (1, 0), (1, 1), (2, 0)),
    ((2, 0), (1, 0), (3, 1), (0, 0), (0, 1), (1, 1), (2, 1), (3, 0)),
)


def dot(a, b, dims=((1,), (0,)), precision=HIGH):
    return lax.dot_general(a, b, (dims, ((), ())), precision=precision, preferred_element_type=F32)


def bdot(a, b, dims=((1,), (0,))):
    return lax.dot_general(a, b, (dims, ((), ())), preferred_element_type=F32)


def channel_norm(x):
    centre = x - jnp.mean(x, axis=-1, keepdims=True)
    return centre * lax.rsqrt(jnp.mean(centre * centre, axis=-1, keepdims=True) + EPS)


def ksplit(x):
    high = x.astype(BF)
    return high, (x - high.astype(F32)).astype(BF)


def merge_kernel(group, parts_ref, out_ref):
    sources, _, lanes = parts_ref.shape
    rows = out_ref.shape[1]
    tops = [parts_ref[s, rows : rows + group, :] for s in range(sources)]
    top = functools.reduce(jnp.maximum, tops)
    scales = [jnp.exp(t - top) for t in tops]
    total = sum(parts_ref[s, rows + group :, :] * scales[s] for s in range(sources))
    factors = jnp.concatenate([x / total for x in scales], axis=0)
    factors = jnp.concatenate([factors, jnp.zeros((lanes - sources * group, lanes), F32)], axis=0)
    factors = jnp.transpose(factors)[:rows]
    head = lax.broadcasted_iota(jnp.int32, (rows, lanes), 1) // (lanes // group)
    attn = jnp.zeros((rows, lanes), F32)
    for s in range(sources):
        factor = factors[:, s * group : s * group + 1]
        for h in range(1, group):
            factor = jnp.where(head == h, factors[:, s * group + h : s * group + h + 1], factor)
        attn = attn + parts_ref[s, :rows, :] * factor
    for s in range(sources):
        out_ref[s] = attn


def project_kernel(attn_ref, w_out_ref, seq_ref, w_left_ref, w_right_ref, seq_new_ref, out_ref):
    sources, rows, lanes = attn_ref.shape
    attn = jnp.concatenate([attn_ref[s] for s in range(sources)], axis=1)
    both = bdot(jnp.concatenate(ksplit(attn), axis=0), jnp.concatenate(ksplit(w_out_ref[...]), axis=1))
    both = both[:, :lanes] + both[:, lanes:]
    total = seq_ref[...] + (both[:rows] + both[rows:])
    seq_new_ref[...] = total
    w_lr = jnp.concatenate([w_left_ref[...], w_right_ref[...]], axis=0)
    part = dot(total, w_lr, ((1,), (1,)))
    ones = jnp.ones((8, lanes), F32)
    sums = dot(ones, total, ((1,), (1,)))
    squares = dot(ones, total * total, ((1,), (1,)))
    row = lax.broadcasted_iota(jnp.int32, (8, rows), 0)
    stats = jnp.where(row == 0, sums, squares)
    columns = dot(ones, w_lr, ((1,), (1,)))[:1]
    for s in range(out_ref.shape[0]):
        out_ref[s, :rows, :] = part
        out_ref[s, rows : rows + 8, :] = jnp.zeros((8, lanes), F32)
        out_ref[s, rows : rows + 2, :rows] = stats[:2]
        out_ref[s, rows + 2 : rows + 3, :] = columns


def left_right_kernel(width, parts_ref, left_ref, right_ref):
    sources = parts_ref.shape[0]
    rows, lanes = left_ref.shape
    total = parts_ref[0]
    for s in range(1, sources):
        total = total + parts_ref[s]
    stats = jnp.transpose(total[rows : rows + 8, :])
    mean = stats[:rows, 0:1] / width
    square = stats[:rows, 1:2] / width
    both = (total[:rows] - mean * total[rows + 2 : rows + 3]) * lax.rsqrt(square - mean * mean + EPS)
    swapped = pltpu.roll(both, lanes // 2, 1)
    first = lax.broadcasted_iota(jnp.int32, (rows, lanes), 1) < lanes // 2
    left_ref[...] = jnp.where(first, both, swapped)
    right = jnp.where(first, swapped, both)
    right_ref[...] = jnp.where(first[: rows // 2], right[: rows // 2], right[rows // 2 :])


def pack_kernel(key_ref, value_ref, kv_ref):
    lanes = kv_ref.shape[2]
    tails = jnp.concatenate([key_ref[:, lanes:], value_ref[:, lanes:]], axis=1)
    packed = jnp.concatenate([key_ref[:, :lanes], value_ref[:, :lanes], tails], axis=0)
    for s in range(kv_ref.shape[0]):
        kv_ref[s] = packed


def bias_kernel(pair_ref, w_ref, out_ref, done_ref):
    heads, steps, _ = out_ref.shape
    done_ref[...] = jnp.zeros(done_ref.shape, F32)
    w = jnp.concatenate([jnp.concatenate([x, x], axis=1) for x in ksplit(w_ref[...])], axis=0)
    for r in range(steps):
        high, low = ksplit(channel_norm(pair_ref[r]))
        both = bdot(w, jnp.concatenate([high, low], axis=1), ((1,), (1,)))
        out_ref[:, r, :] = both[:heads] + both[heads:]


def pair_bias(pair, w_bias):
    rows, cols, channels = pair.shape
    heads = w_bias.shape[1]
    w = w_bias.T
    block = pl.BlockSpec((BIAS_ROWS, cols, channels), lambda s: (s, 0, 0))
    return pl.pallas_call(
        bias_kernel,
        grid=(rows // BIAS_ROWS,),
        in_specs=[
            block,
            pl.BlockSpec(w.shape, lambda s: (0, 0)),
        ],
        out_specs=(
            pl.BlockSpec((heads, BIAS_ROWS, cols), lambda s: (0, s, 0)),
            pl.BlockSpec((8, 128), lambda s: (0, 0)),
        ),
        out_shape=(jax.ShapeDtypeStruct((heads, rows, cols), F32), jax.ShapeDtypeStruct((8, 128), F32)),
        compiler_params=pltpu.CompilerParams(vmem_limit_bytes=24 * MIB),
        cost_estimate=pl.CostEstimate(
            flops=12 * rows * cols * channels * heads,
            bytes_accessed=4 * rows * cols * (channels + heads),
            transcendentals=rows * cols,
        ),
        name="pair_bias",
    )(pair, w)


def attention_kernel(place_ref, q_ref, far_ref, own_ref, other_ref, bias_ref, out_ref):
    rows, lanes = q_ref.shape[1:]
    cols = bias_ref.shape[2]
    steps = out_ref.shape[0]
    group = bias_ref.shape[0] // steps
    hd = lanes // group
    even = place_ref[0] == 0
    scale = 1.0 / hd**0.5
    lane = lax.broadcasted_iota(jnp.int32, (rows, lanes), 1)
    for g in range(steps):
        heads = []
        for p in range(g * group // 2, (g + 1) * group // 2):
            own, other = own_ref[p], other_ref[p]
            heads += [jnp.where(even, own, other), jnp.where(even, other, own)]
        tails = jnp.concatenate([x[2 * hd :] for x in heads], axis=0)
        keys = jnp.concatenate([x[:hd] for x in heads], axis=0)
        keys = jnp.concatenate([keys, tails[:, : lanes // 2]], axis=1)
        values = jnp.concatenate([x[hd : 2 * hd] for x in heads], axis=0)
        values = jnp.concatenate([values, tails[:, lanes // 2 :]], axis=1)
        k_high, k_low = ksplit(keys)
        v_high, v_low = ksplit(values)
        slot = g ^ place_ref[1]
        near = slot < q_ref.shape[0]
        slot = lax.rem(slot, q_ref.shape[0])
        q = jnp.where(near, q_ref[slot], far_ref[slot]) * scale
        q = jnp.concatenate([jnp.where(lane // hd == h, q, 0.0) for h in range(group)], axis=0)
        q = jnp.concatenate(ksplit(q), axis=1)
        scores = bdot(q, jnp.concatenate([k_high, k_high], axis=0)) + bdot(q, jnp.concatenate([k_low, k_low], axis=0))
        scores = scores + bias_ref[g * group : (g + 1) * group].reshape(group * rows, cols)
        top = jnp.max(scores, axis=1, keepdims=True)
        expo = jnp.exp(scores - top)
        total = jnp.sum(expo, axis=1, keepdims=True)
        w = bdot(
            jnp.concatenate(ksplit(expo), axis=0), jnp.concatenate([v_high, v_low], axis=0), ((1,), (1,))
        )
        half = group * rows
        w = (w[:half, :lanes] + w[:half, lanes:]) + (w[half:, :lanes] + w[half:, lanes:])
        weighted = jnp.zeros((rows, lanes), F32)
        stats = jnp.zeros((rows, lanes), F32)
        for h in range(group):
            part = slice(h * rows, (h + 1) * rows)
            weighted = jnp.where(lane // hd == h, w[part], weighted)
            stats = jnp.where(lane == h, top[part], stats)
            stats = jnp.where(lane == h + group, total[part], stats)
        out_ref[g, :rows, :] = weighted
        stats = jnp.concatenate([stats, jnp.zeros((lanes - rows, lanes), F32)], axis=0)
        out_ref[g, rows:, :] = jnp.transpose(stats)[: 2 * group]


def attention(place, queries, far_queries, own, other, bias):
    n_col, rows, lanes = 2 * queries.shape[0], *queries.shape[1:]
    heads, _, cols = bias.shape
    group = heads // n_col
    return pl.pallas_call(
        attention_kernel,
        in_specs=[pl.BlockSpec(memory_space=pltpu.SMEM)] + [pl.BlockSpec(memory_space=pltpu.VMEM)] * 5,
        out_shape=jax.ShapeDtypeStruct((n_col, rows + 2 * group, lanes), F32),
        compiler_params=pltpu.CompilerParams(vmem_limit_bytes=24 * MIB),
        name="attention",
    )(place, queries, far_queries, own, other, bias)


def update_kernel(
    place_ref, pair_ref, left_ref, own_ref, other_ref, w_outer_ref, bias_ref, w_up_ref, w_down_ref, out_ref,
    rights, base, diffs, w_prod, w_ups, w_downs, pairs, news, loaded, stored,
):
    rows, _, lanes = pair_ref.shape
    starts = range(0, rows, CHUNK_ROWS)

    def chunk(start):
        return pl.ds(start, CHUNK_ROWS)

    loads = [
        pltpu.make_async_copy(pair_ref.at[chunk(s)], pairs.at[chunk(s)], loaded.at[k]) for k, s in enumerate(starts)
    ]
    stores = [
        pltpu.make_async_copy(news.at[chunk(s)], out_ref.at[chunk(s)], stored.at[k]) for k, s in enumerate(starts)
    ]
    for load in loads:
        load.start()

    w_diff = w_outer_ref[lanes // 2 :, :]
    half = own_ref.shape[1]
    first = lax.broadcasted_iota(jnp.int32, (half, lanes), 1) < lanes // 2
    even = place_ref[0] == 0
    blocks = []
    for p in range(rights.shape[0] // (4 * half)):
        own, other = own_ref[p], other_ref[p]
        blocks += [jnp.where(even, own, other), jnp.where(even, other, own)]
    for block, packed in enumerate(blocks):
        swapped = pltpu.roll(packed, lanes // 2, 1)
        start = 2 * half * block
        rights[start : start + half, :] = jnp.where(first, packed, swapped)
        rights[start + half : start + 2 * half, :] = jnp.where(first, swapped, packed)
    base[...] = bias_ref[...] - dot(rights[:, : lanes // 2], w_diff)
    diffs[...] = dot(left_ref[:, : lanes // 2], w_diff)
    high, low = ksplit(w_outer_ref[: lanes // 2, :])
    w_prod[...] = jnp.concatenate([high, high, low, low], axis=0)
    high, low = ksplit(w_up_ref[...])
    w_ups[...] = jnp.concatenate([high, high, low, low], axis=0)
    both = jnp.concatenate(ksplit(w_down_ref[...]), axis=1)
    w_downs[...] = jnp.concatenate([both, both], axis=0)

    first = lax.broadcasted_iota(jnp.int32, base.shape, 1) < lanes // 2

    def normalize(start):
        products, mid = [], []
        loads[start // CHUNK_ROWS].wait()
        for i in range(start, start + CHUNK_ROWS):
            product = rights[...] * left_ref[i : i + 1, :]
            high = product.astype(BF).astype(F32)
            products.append(jnp.where(first, high, product - high).astype(BF))
            mid.append(pairs[i] + (base[...] + diffs[i : i + 1, :]))
        products = jnp.concatenate(products, axis=0)
        mid = jnp.concatenate(mid, axis=0) + bdot(jnp.concatenate([products, products], axis=1), w_prod[...])
        high, low = ksplit(channel_norm(mid))
        return mid, jnp.concatenate([high, low, high, low], axis=1)

    def transition(start, mid, normed):
        hidden = ksplit(jnp.maximum(bdot(normed, w_ups[...]), 0.0))
        down = bdot(jnp.concatenate(hidden, axis=1), w_downs[...])
        out = mid + (down[:, :lanes] + down[:, lanes:])
        news[start : start + CHUNK_ROWS] = out.reshape((CHUNK_ROWS,) + out_ref.shape[1:])
        stores[start // CHUNK_ROWS].start()

    current = normalize(0)
    for start in starts:
        following = normalize(start + CHUNK_ROWS) if start + CHUNK_ROWS < rows else None
        transition(start, *current)
        current = following
    for store in stores:
        store.wait()


def update_pair(place, pair, left, rights, w_outer, outer_bias, w_up, w_down):
    rows, cols, channels = pair.shape
    hidden = w_up.shape[1]
    whole = lambda x: pl.BlockSpec(x.shape, lambda s: (0,) * x.ndim)
    block = pl.BlockSpec(memory_space=pl.ANY)
    fixed = (left, *rights, w_outer, outer_bias[None, :], w_up, w_down)
    cells = rows * cols
    return pl.pallas_call(
        update_kernel,
        grid=(1,),
        in_specs=[pl.BlockSpec(memory_space=pltpu.SMEM), block] + [whole(x) for x in fixed],
        out_specs=block,
        out_shape=jax.ShapeDtypeStruct(pair.shape, F32),
        scratch_shapes=[
            pltpu.VMEM((cols, channels), F32),
            pltpu.VMEM((cols, channels), F32),
            pltpu.VMEM((rows, channels), F32),
            pltpu.VMEM((2 * w_outer.shape[0], channels), BF),
            pltpu.VMEM((4 * channels, hidden), BF),
            pltpu.VMEM((2 * hidden, 2 * channels), BF),
            pltpu.VMEM(pair.shape, F32),
            pltpu.VMEM(pair.shape, F32),
            pltpu.SemaphoreType.DMA((rows // CHUNK_ROWS,)),
            pltpu.SemaphoreType.DMA((rows // CHUNK_ROWS,)),
        ],
        compiler_params=pltpu.CompilerParams(vmem_limit_bytes=57 * MIB),
        cost_estimate=pl.CostEstimate(
            flops=2 * cells * channels * (8 * hidden + 256),
            bytes_accessed=8 * cells * channels,
            transcendentals=cells,
        ),
        name="update_pair",
    )(place, pair, *fixed)


def after(x, *others):
    place = pl.BlockSpec(memory_space=pl.ANY)
    return pl.pallas_call(
        lambda *refs: None,
        in_specs=[place] * (1 + len(others)),
        out_specs=place,
        out_shape=jax.ShapeDtypeStruct(x.shape, x.dtype),
        input_output_aliases={0: 0},
        compiler_params=pltpu.CompilerParams(vmem_limit_bytes=MIB),
        name="after",
    )(x, *others)


def columns_first(n_row, n_col, other):
    pairs = []
    for k in range(n_col):
        for half in range(2):
            for core in range(2):
                for plane in range(n_row // 4):
                    x, y = HOPS[other][(plane - k) % (n_row // 4)]
                    source = ((k // 2 + x) % (n_col // 2)) * 2 + ((k % 2) ^ y)
                    pairs.append(
                        (((k * 2 + (half ^ other)) * 2 + core) * n_col + source, ((plane * 2 + half) * 2 + core) * n_col + k)
                    )
    return sorted(pairs)


def per_device(
    seq, query, key, value, pair, w_bias, w_out, w_left, w_right, w_outer, outer_bias, w_up, w_down
):
    rows, cols, channels = pair.shape
    heads = w_bias.shape[1]
    width = w_out.shape[0]
    head_dim = width // heads
    n_row, n_col = lax.axis_size("row"), lax.axis_size("col")
    group = heads // n_col

    kv = pl.pallas_call(
        pack_kernel,
        out_shape=jax.ShapeDtypeStruct((n_row // 2, 3 * head_dim, channels), F32),
        name="pack",
    )(key.T, value.T)
    queries = query[None]
    hop = 1
    while hop < n_col:
        if hop > 1:
            queries = jnp.concatenate([queries, far_queries], axis=0)
        far_queries = lax.ppermute(queries, "col", [(i, i ^ hop) for i in range(n_col)])
        hop *= 2
    pairs = [[z * 2 + k for z in range(n_row // 2)] for k in range(2)]
    own = lax.all_to_all(kv, "row", 0, 0, axis_index_groups=pairs)
    bias, bias_done = pair_bias(pair, w_bias)
    own = after(own, far_queries[:1, :8], bias_done)
    across = [(i, i ^ 1) for i in range(n_row)]
    other = lax.ppermute(own, "row", across)
    place = jnp.stack([lax.axis_index("row") % 2, lax.axis_index("col")])
    parts = attention(place, queries, far_queries, own, other, bias)
    parts = lax.all_to_all(parts, "col", 0, 0)

    attn = pl.pallas_call(
        functools.partial(merge_kernel, group),
        out_shape=jax.ShapeDtypeStruct((n_col, rows, channels), F32),
        compiler_params=pltpu.CompilerParams(vmem_limit_bytes=8 * MIB),
        name="merge",
    )(parts)
    attn = lax.all_to_all(attn, "col", 0, 0)
    seq_new, shares = pl.pallas_call(
        project_kernel,
        out_shape=(
            jax.ShapeDtypeStruct(seq.shape, F32),
            jax.ShapeDtypeStruct((n_col, rows + 8, channels), F32),
        ),
        compiler_params=pltpu.CompilerParams(vmem_limit_bytes=8 * MIB),
        name="project",
    )(attn, w_out, seq, w_left.T, w_right.T)
    shares = lax.all_to_all(shares, "col", 0, 0)
    left, right = pl.pallas_call(
        functools.partial(left_right_kernel, width),
        out_shape=(
            jax.ShapeDtypeStruct((rows, channels), F32),
            jax.ShapeDtypeStruct((rows // 2, channels), F32),
        ),
        compiler_params=pltpu.CompilerParams(vmem_limit_bytes=8 * MIB),
        name="left_right",
    )(shares)
    near, far = [lax.ppermute(right, ("row", "col"), columns_first(n_row, n_col, other)) for other in (0, 1)]
    second = lax.axis_index("row") // 2 % 2 == 1
    right = jnp.stack([jnp.where(second, far, near), jnp.where(second, near, far)])
    rights = (right, lax.ppermute(right, "row", across))
    return seq_new, update_pair(place, pair, left, rights, w_outer, outer_bias, w_up, w_down)


def solution(mesh):
    in_specs = (
        P("row", "col"),
        P("row", "col"),
        P("col", "row"),
        P("col", "row"),
        P("row", "col", None),
        P(),
        P(None, "col"),
        P("col", None),
        P("col", None),
        P(),
        P(),
        P(),
        P(),
    )
    out_specs = (P("row", "col"), P("row", "col", None))
    return jax.shard_map(
        per_device, mesh=mesh, in_specs=in_specs, out_specs=out_specs, check_vma=False
    )
```
